128 devices in a mesh: dp: 8 (over y, core), fsdp: 16 (over x, z).
Axes of the slice: x: 4, y: 4, z: 4, core: 2. Of those that a mesh axis runs over, the one named last changes fastest.
Arguments:
- activations: bfloat16 [114688, 8192], P(('dp', 'fsdp')), may hold values from -6 to 6
- key_cotangent: bfloat16 [114688, 1024], P(('dp', 'fsdp')), may hold values from -0.046875 to 0.046875
- momentum: float32 [8, 8192, 1024], P('dp', 'fsdp'), may hold values from -6 to 6
- frequencies: int32 [8, 128, 16, 32], P('dp', 'fsdp'), may hold values from 0 to 4095, all different within a row
Outputs:
- update: float32 [8192, 1024], P('fsdp')
- new_momentum: float32 [8, 8192, 1024], P('dp', 'fsdp')
The draws below stay inside these ranges and needn't reach their ends.
Inputs may be any that keep to these rules, and one draw needn't show every extreme that they name: The 32 frequencies of one tile and replica are all different.
All inputs are finite; a program needn't handle non-finite values.
Results may differ from the reference program's by a relative error of at most 0.0003.
Values may be sent and summed in bfloat16 or wider, within the bound.
No kernel may reach another device: no remote copies, remote signals or barrier semaphores. Data moves between devices by JAX's collectives and lax.ppermute only.
A program may use at most 192 MiB of HBM per device.

```python
import jax
import jax.numpy as jnp
from jax import lax

D = 8192
KV = 1024
TOK_DEV = 896
TILE = 64
PICK = 32
TOKENS = 114688
N_DP = 8
N_FSDP = 16


def block_scale(own_key, shape, shards, least, top_value):
    loudness = 1.0
    for dim, shards_of in shards:
        steps = jax.random.uniform(jax.random.fold_in(jax.random.fold_in(own_key, 6), dim), (shards_of,), jnp.float32, least / len(shards), top_value / len(shards))
        loudness = loudness * jnp.repeat(jnp.exp(steps), shape[dim] // shards_of).reshape((-1,) + (1,) * (len(shape) - 1 - dim))
    return loudness


def picks_of(own_key, rows, number_of, top, lift):
    ranking = jax.random.permutation(jax.random.fold_in(own_key, 1), number_of)
    pull = ranking
    for power in range(3):
        pull = pull * pull // number_of
    pull = pull * lift // number_of
    chance = jax.random.randint(jax.random.fold_in(own_key, 2), (rows, number_of), 0, 4096) + pull
    fixed_rows = jax.random.permutation(jax.random.fold_in(own_key, 3), rows)[jnp.arange(number_of) % rows]
    chance = jnp.where(jnp.arange(rows)[:, None] == fixed_rows[None, :], 1 << 14, chance)
    priority = chance * number_of + jnp.arange(number_of)
    return lax.top_k(priority.astype(jnp.int32), top)[1].astype(jnp.int32)


def centred(stream_key, extent, spread, most, split=(), held_as=jnp.bfloat16):
    array = jax.random.normal(stream_key, extent, jnp.float32) * spread
    if len(split) > 0:
        array = block_scale(stream_key, extent, split, -0.22, 0.18) * array
    return jnp.clip(array, min=-most, max=most).astype(held_as)


def setup_inputs(seed: int = 0) -> dict:
    arg_keys = jax.random.split(jax.random.key(seed), 5)
    activations = centred(arg_keys[0], (TOKENS, D), 1.0, 6.0, ((0, 128),))
    key_cotangent = centred(arg_keys[1], (TOKENS, KV), (TOK_DEV * N_FSDP) ** -0.5, 0.046875, ((0, 128),))
    momentum = centred(arg_keys[2], (N_DP, D, KV), 1.0, 6.0, ((0, 8), (1, 16)), jnp.float32)
    frequencies = picks_of(arg_keys[3], N_DP * (D // TILE) * (KV // TILE), TILE * TILE, PICK, 0).reshape((N_DP, D // TILE, KV // TILE, PICK))
    return {"activations": activations, "key_cotangent": key_cotangent, "momentum": momentum, "frequencies": frequencies}


momentum_decay = 0.999

def cosine_table():
    freq_rows = jnp.arange(TILE, dtype=jnp.float32)[:, None]
    positions = jnp.arange(TILE, dtype=jnp.float32)[None, :]
    cosine = jnp.cos(jnp.pi * (2.0 * positions + 1.0) * freq_rows / (2.0 * TILE)) * jnp.sqrt(2.0 / TILE)
    scaling = jnp.where(jnp.arange(TILE) == 0, jnp.sqrt(0.5), 1.0).astype(jnp.float32)
    return cosine * scaling[:, None]

def forward_tiles(matrix, cosine):
    row_count, col_count = matrix.shape
    flat = matrix.reshape(row_count * (col_count // TILE), TILE)
    half = jnp.dot(flat, cosine.T, precision=lax.Precision.HIGHEST).reshape(row_count // TILE, TILE, col_count // TILE, TILE)
    return jnp.einsum('kn,anbl->abkl', cosine, half, precision=lax.Precision.HIGHEST)

def inverse_tiles(spectra, cosine):
    half = jnp.einsum('kn,abkl->abnl', cosine, spectra, precision=lax.Precision.HIGHEST)
    dense_part = jnp.einsum('abnl,lm->anbm', half, cosine, precision=lax.Precision.HIGHEST)
    shape_a, shape_n, shape_b, shape_m = dense_part.shape
    return dense_part.reshape(shape_a * shape_n, shape_b * shape_m)

def extract(spectra, chosen):
    tiles_a, tiles_b = (spectra.shape[0], spectra.shape[1])
    flat = spectra.reshape(tiles_a, tiles_b, TILE * TILE)
    return jnp.take_along_axis(flat, chosen, axis=2)

def place(values, chosen):
    tiles_a, tiles_b = (values.shape[0], values.shape[1])
    index_a = jnp.arange(tiles_a, dtype=jnp.int32)[:, None, None]
    index_b = jnp.arange(tiles_b, dtype=jnp.int32)[None, :, None]
    flat = jnp.zeros((tiles_a, tiles_b, TILE * TILE), jnp.float32).at[index_a, index_b, chosen].add(values)
    return flat.reshape(tiles_a, tiles_b, TILE, TILE)

def reference(activations, key_cotangent, momentum, frequencies):
    cosine = cosine_table()
    update = jnp.zeros((D, KV), jnp.float32)
    moments_out = []
    for group in range(N_DP):

        def accumulate(running, member):
            first_row = group * N_FSDP * TOK_DEV + member * TOK_DEV
            token_part = lax.dynamic_slice_in_dim(activations, first_row, TOK_DEV, 0)
            cot_part = lax.dynamic_slice_in_dim(key_cotangent, first_row, TOK_DEV, 0)
            partial_value = lax.dot_general(token_part, cot_part, (((0,), (0,)), ((), ())), preferred_element_type=jnp.float32)
            return (running + partial_value, None)
        gradient, unused = lax.scan(accumulate, jnp.zeros((D, KV), jnp.float32), jnp.arange(N_FSDP, dtype=jnp.int32))
        moment = momentum_decay * momentum[group] + gradient
        spectra = forward_tiles(moment, cosine)
        values = extract(spectra, frequencies[group])
        removed = inverse_tiles(place(values, frequencies[group]), cosine)
        update = update + removed
        moments_out.append(moment - removed)
    return (update / N_DP, jnp.stack(moments_out))
```

```python
import functools

import jax
import jax.numpy as jnp
import ml_dtypes
import numpy as np
from jax import lax
from jax.experimental import pallas as pl
from jax.experimental.pallas import tpu as pltpu
from jax.sharding import PartitionSpec as P

EDGE = 64
PICK = 32
DECAY = 0.999
RING = 4
ORDER = (2, 1, 3, 0)
GROUPS = 16
VMEM = 56 * 1024 * 1024
F32 = jnp.float32
BF16 = jnp.bfloat16


def params():
    return pltpu.CompilerParams(vmem_limit_bytes=VMEM)


def cosine_matrix():
    k = np.arange(EDGE)[:, None]
    n = np.arange(EDGE)[None, :]
    c = np.sqrt(2.0 / EDGE) * np.cos(np.pi * (2 * n + 1) * k / (2 * EDGE))
    c[0] = np.sqrt(1.0 / EDGE)
    return c


def split_table(table):
    hi = table.astype(ml_dtypes.bfloat16)
    lo = (table - hi.astype(np.float64)).astype(ml_dtypes.bfloat16)
    return np.stack([hi, lo])


def dot(a, b):
    return jnp.dot(a, b, preferred_element_type=F32)


def halves(a):
    hi = a.astype(BF16)
    return hi, (a - hi.astype(F32)).astype(BF16)


def dot_right(a, table):
    hi, lo = halves(a)
    return dot(hi, table[0]) + (dot(hi, table[1]) + dot(lo, table[0]))


def dot_left(table, a):
    hi, lo = halves(a)
    return dot(table[0], hi) + (dot(table[1], hi) + dot(table[0], lo))


def encode(value, out_ref, lanes=slice(None)):
    rows = value.shape[0]
    step = rows // GROUPS
    cube = value.reshape(GROUPS, step, value.shape[1])
    most = jnp.maximum(jnp.max(jnp.abs(cube), axis=1), 1e-30)
    power = jnp.ceil(256.0 * jnp.log2(most) + 0.5)
    inverse = 32767.0 * jnp.exp2(power * (-1.0 / 256.0))
    code = jnp.floor(cube * inverse[:, None, :] + 0.5).astype(jnp.int32).astype(jnp.int16)
    out_ref[:rows, lanes] = code.reshape(rows, value.shape[1])
    out_ref[rows:, lanes] = power.astype(jnp.int32).astype(jnp.int16)


def decode(ref, lanes=slice(None)):
    rows = ref.shape[0] - GROUPS
    step = rows // GROUPS
    scale = jnp.exp2(ref[rows:, lanes].astype(jnp.int32).astype(F32) * (1.0 / 256.0)) * (1.0 / 32767.0)
    code = ref[:rows, lanes].astype(jnp.int32).astype(F32)
    width = code.shape[1]
    return (code.reshape(GROUPS, step, width) * scale[:, None, :]).reshape(rows, width)


def matmul_kernel(modes, idx_ref, kt_ref, act_ref, *out_refs):
    product = dot(kt_ref[...], act_ref[...])
    if modes == "own":
        out_refs[0][...] = product
        return
    for half, coded in enumerate(modes):
        part = product[:, half * 128 : (half + 1) * 128]
        if coded:
            encode(part, out_refs[half])
        else:
            out_refs[half][...] = part


def matmul(kt, act, idx, modes):
    kv, tokens = kt.shape
    if modes == "own":
        shapes = [jax.ShapeDtypeStruct((kv, 1024), F32)]
        specs = [pl.BlockSpec((kv, 256), lambda i, idx: (0, i))]
    else:
        shapes = [
            jax.ShapeDtypeStruct((kv + GROUPS, 512), jnp.int16) if c else jax.ShapeDtypeStruct((kv, 512), F32)
            for c in modes
        ]
        specs = [pl.BlockSpec((s.shape[0], 128), lambda i, idx: (0, i)) for s in shapes]
    return pl.pallas_call(
        functools.partial(matmul_kernel, modes),
        out_shape=shapes,
        grid_spec=pltpu.PrefetchScalarGridSpec(
            num_scalar_prefetch=1,
            grid=(4,),
            in_specs=[
                pl.BlockSpec((kv, tokens), lambda i, idx: (0, 0)),
                pl.BlockSpec((tokens, 256), lambda i, idx: (0, idx[i])),
            ],
            out_specs=specs,
        ),
        compiler_params=params(),
        cost_estimate=pl.CostEstimate(
            flops=2 * kv * tokens * 1024, bytes_accessed=6 * 1024 * 1024, transcendentals=0
        ),
    )(idx, kt, act)


def merge_kernel(own_ref, got_ref, out_ref):
    encode(own_ref[...] + decode(got_ref), out_ref)


def merge(own, got):
    rows, cols = own.shape
    wide = pl.BlockSpec((rows + GROUPS, 128), lambda i: (0, i))
    return pl.pallas_call(
        merge_kernel,
        out_shape=jax.ShapeDtypeStruct((rows + GROUPS, cols), jnp.int16),
        grid=(cols // 128,),
        in_specs=[pl.BlockSpec((rows, 128), lambda i: (0, i)), wide],
        out_specs=wide,
        compiler_params=params(),
        cost_estimate=pl.CostEstimate(flops=8 * rows * cols, bytes_accessed=8 * rows * cols, transcendentals=0),
    )(own, got)


def combine_kernel(modes, own_ref, a0, b0, a1, b1, *out_refs):
    for half, (a, b) in enumerate(((a0, b0), (a1, b1))):
        total = own_ref[:, half * 128 : (half + 1) * 128] + (decode(a) + decode(b))
        if modes[half]:
            encode(total, out_refs[half])
        else:
            out_refs[half][...] = total


def combine(own, got, spot, modes):
    rows = own.shape[0]
    shapes = [
        jax.ShapeDtypeStruct((rows + GROUPS, 128), jnp.int16) if c else jax.ShapeDtypeStruct((rows, 128), F32)
        for c in modes
    ]
    wide = pl.BlockSpec((rows + GROUPS, 128), lambda i: (0, spot))
    return pl.pallas_call(
        functools.partial(combine_kernel, modes),
        out_shape=shapes,
        grid=(1,),
        in_specs=[pl.BlockSpec((rows, 256), lambda i: (0, spot))] + [wide] * 4,
        out_specs=[pl.BlockSpec(s.shape, lambda i: (0, 0)) for s in shapes],
        compiler_params=params(),
        cost_estimate=pl.CostEstimate(flops=rows * 2048, bytes_accessed=rows * 3072, transcendentals=0),
    )(own, *got)


def pick_rows(freq_ref, b, half):
    chosen = freq_ref[b : b + 1, half * 128 : (half + 1) * 128]
    return chosen // EDGE, chosen % EDGE


def place_matrix(high):
    tile = lax.broadcasted_iota(jnp.int32, (1, 128), 1) // PICK
    rows = lax.broadcasted_iota(jnp.int32, (256, 128), 0)
    return jnp.where(rows == high + tile * EDGE, 1.0, 0.0).astype(BF16)


def spectra_kernel(decayed_ref, right_ref, left_ref, freq_ref, *refs):
    ins, outs = refs[:18], refs[18:]
    moment_ref, spectra_ref, values_ref = outs
    sub = lax.broadcasted_iota(jnp.int32, (EDGE, 128), 0)
    for half in range(2):
        own, early, late = ins[half * 9], ins[half * 9 + 1 : half * 9 + 5], ins[half * 9 + 5 : half * 9 + 9]
        for q in range(2):
            lanes = slice(half * 256 + q * 128, half * 256 + (q + 1) * 128)
            total = own[:, q * 128 : (q + 1) * 128] + (decode(early[2 * q]) + decode(early[2 * q + 1]))
            total = total + (decode(late[2 * q]) + decode(late[2 * q + 1]))
            moment_ref[:, lanes] = decayed_ref[:, lanes] + total
        cols = slice(half * 256, (half + 1) * 256)
        half_done = dot_right(moment_ref[:, cols], right_ref)
        for block in range(4):
            rows = slice(block * 256, (block + 1) * 256)
            spectrum = dot_left(left_ref, half_done[rows])
            spectra_ref[rows, cols] = spectrum
            for inner in range(4):
                b = block * 4 + inner
                high, low = pick_rows(freq_ref, b, half)
                hi, lo = halves(spectrum[inner * EDGE : (inner + 1) * EDGE])
                place = place_matrix(high)
                picked = dot(hi, place) + dot(lo, place)
                values_ref[b : b + 1, half * 128 : (half + 1) * 128] = jnp.sum(
                    jnp.where(sub == low, picked, 0.0), axis=0, keepdims=True
                )


def spectra(decayed, right, left, freq, a, b):
    rows = decayed.shape[0]
    full = lambda s: pl.BlockSpec(s, lambda i: (0,) * len(s))
    block = lambda r, c, j: pl.BlockSpec((r, c), lambda i: (0, j))
    specs = [full(decayed.shape), full(right.shape), full(left.shape), full(freq.shape)]
    operands = [decayed, right, left, freq]
    for own, early, late in (a, b):
        operands += [own, *early, *late]
        specs += [block(rows, 256, 3)] + [block(rows + GROUPS, 128, 3)] * 4 + [block(rows + GROUPS, 128, 0)] * 4
    shapes = [
        jax.ShapeDtypeStruct((rows, 512), F32),
        jax.ShapeDtypeStruct((rows, 512), F32),
        jax.ShapeDtypeStruct((16, 256), F32),
    ]
    return pl.pallas_call(
        spectra_kernel,
        out_shape=shapes,
        grid=(1,),
        in_specs=specs,
        out_specs=[full(s.shape) for s in shapes],
        compiler_params=params(),
        cost_estimate=pl.CostEstimate(flops=10**9, bytes_accessed=16 * 1024 * 1024, transcendentals=0),
    )(*operands)


def remove_kernel(moment_ref, spectra_ref, left_ref, right_ref, freq_ref, out_ref):
    sub = lax.broadcasted_iota(jnp.int32, (EDGE, 128), 0)
    for half in range(2):
        cols = slice(half * 256, (half + 1) * 256)
        for block in range(4):
            rows = slice(block * 256, (block + 1) * 256)
            masks = []
            for inner in range(4):
                high, low = pick_rows(freq_ref, block * 4 + inner, half)
                at_low = jnp.where(sub == low, 1.0, 0.0).astype(BF16)
                masks.append(
                    lax.dot_general(
                        at_low, place_matrix(high), (((1,), (1,)), ((), ())), preferred_element_type=F32
                    )
                )
            kept = spectra_ref[rows, cols] * jnp.concatenate(masks, axis=0)
            removed = dot_right(dot_left(left_ref, kept), right_ref)
            out_ref[0, cols, rows] = (moment_ref[rows, cols] - removed).T


def remove(moment, spectrum, left, right, freq):
    rows, cols = moment.shape
    return pl.pallas_call(
        remove_kernel,
        out_shape=jax.ShapeDtypeStruct((1, cols, rows), F32),
        compiler_params=params(),
        cost_estimate=pl.CostEstimate(flops=10**9, bytes_accessed=6 * 1024 * 1024, transcendentals=0),
    )(moment, spectrum, left, right, freq)


def update_kernel(left_ref, right_ref, *refs):
    lists, (out_ref, values, chosen) = refs[:8], refs[8:]
    step = pl.program_id(0)

    @pl.when(step == 0)
    def _():
        for a in range(8):
            cut = slice(a * PICK, (a + 1) * PICK)
            values[a] = jnp.concatenate([r[:16, cut] for r in lists], axis=1)
            chosen[a] = jnp.concatenate([r[16:, cut] for r in lists], axis=1).astype(jnp.int32)

    sub = lax.broadcasted_iota(jnp.int32, (EDGE, 256), 0)
    for group in range(4):
        strips = []
        for inner_a in range(4):
            a = step * 4 + inner_a
            tiles = []
            for inner_b in range(4):
                b = group * 4 + inner_b
                value = values[a, b : b + 1, :]
                where = chosen[a, b : b + 1, :]
                hi, lo = halves(value)
                hit = sub == where // EDGE
                zero = jnp.zeros((EDGE, 256), F32)
                lhs = jnp.concatenate(
                    [
                        jnp.where(hit, hi.astype(F32), zero).astype(BF16),
                        jnp.where(hit, lo.astype(F32), zero).astype(BF16),
                    ],
                    axis=0,
                )
                rhs = jnp.where(sub == where % EDGE, 1.0, 0.0).astype(BF16)
                both = lax.dot_general(lhs, rhs, (((1,), (1,)), ((), ())), preferred_element_type=F32)
                tiles.append(both[:EDGE] + both[EDGE:])
            strips.append(jnp.concatenate(tiles, axis=1))
        spectrum = jnp.concatenate(strips, axis=0)
        out_ref[:, group * 256 : (group + 1) * 256] = dot_right(dot_left(left_ref, spectrum), right_ref) * 0.125


def update_of(lists, left, right):
    full = lambda s: pl.BlockSpec(s, lambda i: (0,) * len(s))
    return pl.pallas_call(
        update_kernel,
        out_shape=jax.ShapeDtypeStruct((512, 1024), F32),
        grid=(2,),
        in_specs=[full(left.shape), full(right.shape)] + [full((32, 256))] * 8,
        out_specs=pl.BlockSpec((256, 1024), lambda i: (i, 0)),
        scratch_shapes=[pltpu.VMEM((8, 16, 256), F32), pltpu.VMEM((8, 16, 256), jnp.int32)],
        compiler_params=params(),
        cost_estimate=pl.CostEstimate(flops=2 * 10**9, bytes_accessed=3 * 1024 * 1024, transcendentals=0),
    )(left, right, *lists)


def shift(value, axis, by):
    if axis == "x":
        pairs = [(x * 4 + z, (x + by) % 4 * 4 + z) for x in range(4) for z in range(4)]
    else:
        pairs = [(x * 4 + z, x * 4 + (z + by) % 4) for x in range(4) for z in range(4)]
    return lax.ppermute(value, "fsdp", pairs)


def first_stage(kt, act, axis, here, there):
    other = "z" if axis == "x" else "x"

    def blocks(away):
        along = (here + away) % RING
        ids = []
        for turn in ORDER:
            across = (there + turn) % RING
            ids.append(2 * (4 * along + across) if axis == "x" else 2 * (4 * across + along) + 1)
        return jnp.stack(ids).astype(jnp.int32)

    far_up, far_down = matmul(kt, act, blocks(2), (True, True))
    got_up, got_down = shift(far_up, axis, 1), shift(far_down, axis, -1)
    keep_up, alone_up = matmul(kt, act, blocks(1), (False, True))
    alone_down, keep_down = matmul(kt, act, blocks(3), (True, False))
    single_up, single_down = shift(alone_up, axis, 1), shift(alone_down, axis, -1)
    (own,) = matmul(kt, act, blocks(0), "own")
    double_up = shift(merge(keep_up, got_up), axis, 1)
    double_down = shift(merge(keep_down, got_down), axis, -1)
    return other, own, (double_up, single_down, single_up, double_down)


def second_stage(other, own, early):
    far_up, far_down = combine(own, early, 0, (True, True))
    got_up, got_down = shift(far_up, other, 1), shift(far_down, other, -1)
    keep_up, alone_up = combine(own, early, 1, (False, True))
    alone_down, keep_down = combine(own, early, 2, (True, False))
    single_up, single_down = shift(alone_up, other, 1), shift(alone_down, other, -1)
    double_up = shift(merge(keep_up, got_up), other, 1)
    double_down = shift(merge(keep_down, got_down), other, -1)
    return own, early, (double_up, single_down, single_up, double_down)


def exchange(mine):
    partner = lax.ppermute(mine, "dp", [(i, i ^ 1) for i in range(8)])
    out = [mine, partner]
    pair = jnp.concatenate([mine, partner], axis=0)
    for by in (1, 2, 3):
        got = lax.ppermute(pair, "dp", [(y * 2 + c, (y + by) % 4 * 2 + c) for y in range(4) for c in range(2)])
        out += [got[:32], got[32:]]
    return out


def per_device(activations, key_cotangent, momentum, frequencies):
    place = lax.axis_index("fsdp")
    x, z = place // RING, place % RING
    kt = key_cotangent.T
    cosine = cosine_matrix()
    by_c = jnp.asarray(split_table(np.kron(np.eye(4), cosine)))
    by_ct = jnp.asarray(split_table(np.kron(np.eye(4), cosine.T)))
    decayed = (DECAY * momentum[0]).T
    freq = jnp.transpose(frequencies[0], (1, 0, 2)).reshape(16, 256)
    first_a = first_stage(kt, activations, "x", x, z)
    first_b = first_stage(kt, activations, "z", z, x)
    second_a = second_stage(*first_a)
    second_b = second_stage(*first_b)
    moment, spectrum, values = spectra(decayed, by_ct, by_c, freq, second_a, second_b)
    lists = exchange(jnp.concatenate([values, freq.astype(F32)], axis=0))
    new_momentum = remove(moment, spectrum, by_ct, by_c, freq)
    update = update_of(lists, by_ct, by_c)
    return update, new_momentum


def solution(mesh):
    in_specs = (
        P(("dp", "fsdp"), None),
        P(("dp", "fsdp"), None),
        P("dp", "fsdp", None),
        P("dp", "fsdp", None, None),
    )
    out_specs = (P("fsdp", None), P("dp", "fsdp", None))
    return jax.shard_map(per_device, mesh=mesh, in_specs=in_specs, out_specs=out_specs, check_vma=False)
```

```python
import functools

import jax
import jax.numpy as jnp
import ml_dtypes
import numpy as np
from jax import lax
from jax.experimental import pallas as pl
from jax.experimental.pallas import tpu as pltpu
from jax.sharding import PartitionSpec as P

EDGE = 64
PICK = 32
DECAY = 0.999
RING = 4
ORDER = ((2, 1, 3, 0), (2, 3, 1, 0))
GROUPS = 16
F32 = jnp.float32
BF16 = jnp.bfloat16


def params(mib):
    return pltpu.CompilerParams(vmem_limit_bytes=mib * 2**20)


def cosine_matrix():
    k = np.arange(EDGE)[:, None]
    n = np.arange(EDGE)[None, :]
    c = np.sqrt(2.0 / EDGE) * np.cos(np.pi * (2 * n + 1) * k / (2 * EDGE))
    c[0] = np.sqrt(1.0 / EDGE)
    return c


def split_table(table):
    hi = table.astype(ml_dtypes.bfloat16)
    lo = (table - hi.astype(np.float64)).astype(ml_dtypes.bfloat16)
    return np.stack([hi, lo])


def dot(a, b):
    return jnp.dot(a, b, preferred_element_type=F32)


def halves(a):
    hi = a.astype(BF16)
    return hi, (a - hi.astype(F32)).astype(BF16)


def dot_right(a, table):
    hi, lo = halves(a)
    return dot(hi, table[0]) + (dot(hi, table[1]) + dot(lo, table[0]))


def dot_left(table, a):
    hi, lo = halves(a)
    return dot(table[0], hi) + (dot(table[1], hi) + dot(table[0], lo))


def encode(value, out_ref, lanes=slice(None)):
    rows = value.shape[0]
    step = rows // GROUPS
    cube = value.reshape(GROUPS, step, value.shape[1])
    most = jnp.maximum(jnp.max(jnp.abs(cube), axis=1), 1e-30)
    power = jnp.ceil(256.0 * jnp.log2(most) + 0.5)
    inverse = 32767.0 * jnp.exp2(power * (-1.0 / 256.0))
    code = jnp.floor(cube * inverse[:, None, :] + 0.5).astype(jnp.int32).astype(jnp.int16)
    out_ref[:rows, lanes] = code.reshape(rows, value.shape[1])
    out_ref[rows:, lanes] = power.astype(jnp.int32).astype(jnp.int16)


def decode(ref, lanes=slice(None)):
    rows = ref.shape[0] - GROUPS
    step = rows // GROUPS
    scale = jnp.exp2(ref[rows:, lanes].astype(jnp.int32).astype(F32) * (1.0 / 256.0)) * (1.0 / 32767.0)
    code = ref[:rows, lanes].astype(jnp.int32).astype(F32)
    width = code.shape[1]
    return (code.reshape(GROUPS, step, width) * scale[:, None, :]).reshape(rows, width)


def product(key, blocks):
    both = jnp.concatenate([r[...] for r in blocks], axis=1)
    return lax.dot_general(key, both, (((0,), (0,)), ((), ())), preferred_element_type=F32)


def matmul_kernel(spots, extra, coded, table_ref, key_ref, *refs):
    acts, gots, outs = refs[: 2 * spots], refs[2 * spots : -2], refs[-2:]
    key = key_ref[...]
    for spot in range(spots):
        lanes = slice(spot * 128, (spot + 1) * 128)
        both = product(key, acts[2 * spot : 2 * spot + 2])
        for half in range(2):
            part = both[:, half * 128 : (half + 1) * 128]
            if extra:
                part = part + decode(gots[half], lanes)
            if coded:
                encode(part, outs[half], lanes)
            else:
                outs[half][:, lanes] = part


def matmul(key, act, table, start, positions, got=(), coded=True):
    tokens, kv = key.shape
    first, count = positions
    spots = 2
    steps = count // spots
    out_rows = kv + GROUPS if coded else kv
    wide = lambda rows, shift: pl.BlockSpec((rows, spots * 128), lambda i, t: (0, i + shift))
    column = lambda n: pl.BlockSpec((tokens, 128), lambda i, t: (0, t[start + 2 * first + 2 * spots * i + n]))
    got_specs = [wide(kv + GROUPS, first // spots if g.shape[1] == 512 else 0) for g in got]
    return pl.pallas_call(
        functools.partial(matmul_kernel, spots, bool(got), coded),
        out_shape=[jax.ShapeDtypeStruct((out_rows, count * 128), jnp.int16 if coded else F32)] * 2,
        grid_spec=pltpu.PrefetchScalarGridSpec(
            num_scalar_prefetch=1,
            grid=(steps,),
            in_specs=[pl.BlockSpec((tokens, kv), lambda i, t: (0, 0))]
            + [column(n) for n in range(2 * spots)]
            + got_specs,
            out_specs=[wide(out_rows, 0)] * 2,
        ),
        compiler_params=params(20),
        cost_estimate=pl.CostEstimate(
            flops=2 * kv * tokens * 256 * count, bytes_accessed=count * 2**20, transcendentals=0
        ),
    )(table, key, *[act] * (2 * spots), *got)


def fold_kernel(count, *refs):
    owns, gots, outs = refs[:2], refs[2:-2], refs[-2:]
    for half in range(2):
        total = owns[half][...]
        for g in gots[half * count : (half + 1) * count]:
            total = total + decode(g)
        encode(total, outs[half])


def fold(own, spot, gots):
    rows = own[0].shape[0]
    count = len(gots[0])
    at = lambda r, j: pl.BlockSpec((r, 128), lambda i: (0, j))
    flat = [g for half in gots for g in half]
    return pl.pallas_call(
        functools.partial(fold_kernel, count),
        out_shape=[jax.ShapeDtypeStruct((rows + GROUPS, 128), jnp.int16)] * 2,
        grid=(1,),
        in_specs=[at(rows, spot)] * 2 + [at(rows + GROUPS, j) for _, j in flat],
        out_specs=[at(rows + GROUPS, 0)] * 2,
        compiler_params=params(12),
        cost_estimate=pl.CostEstimate(flops=rows * 2048, bytes_accessed=rows * 3072, transcendentals=0),
    )(*own, *[g for g, _ in flat])


def pick_rows(freq_ref, b, half):
    chosen = freq_ref[b : b + 1, half * 128 : (half + 1) * 128]
    return chosen >> 6, chosen & 63


def place_matrix(high):
    tile = lax.broadcasted_iota(jnp.int32, (1, 128), 1) // PICK
    rows = lax.broadcasted_iota(jnp.int32, (256, 128), 0)
    return jnp.where(rows == high + tile * EDGE, 1.0, 0.0).astype(BF16)


def spectra_kernel(decayed_ref, right_ref, left_ref, freq_ref, *refs):
    owns, gots, scales = refs[:4], refs[4:16], refs[16:28]
    moment_ref, spectra_ref, values_ref, scale = refs[28:]
    step = pl.program_id(0)

    @pl.when(step == 0)
    def _():
        for j, s in enumerate(scales):
            unit = jnp.exp2(s[...].astype(jnp.int32).astype(F32) * (1.0 / 256.0)) * (1.0 / 32767.0)
            for c in range(4):
                scale[c, j, 0:4, :] = unit[4 * c : 4 * c + 4]

    sub = lax.broadcasted_iota(jnp.int32, (EDGE, 128), 0)
    chosen = freq_ref[0]
    found = []
    for half in range(2):
        parts = []
        for q in range(2):
            block = 2 * half + q
            total = owns[block][...]
            for j in range(3 * block, 3 * block + 3):
                code = gots[j][...].astype(jnp.int32).astype(F32).reshape(4, EDGE, 128)
                total = total + (code * scale[step, j, 0:4, :][:, None, :]).reshape(256, 128)
            lanes = slice(block * 128, (block + 1) * 128)
            parts.append(decayed_ref[:, lanes] + total)
        cols = slice(half * 256, (half + 1) * 256)
        moment = jnp.concatenate(parts, axis=1)
        moment_ref[:, cols] = moment
        spectrum = dot_left(left_ref, dot_right(moment, right_ref))
        spectra_ref[:, cols] = spectrum
        hi, lo = halves(spectrum)
        rows = []
        for inner in range(4):
            line = chosen[inner : inner + 1, half * 128 : (half + 1) * 128]
            place = place_matrix(line >> 6)
            tile = slice(inner * EDGE, (inner + 1) * EDGE)
            picked = dot(hi[tile], place) + dot(lo[tile], place)
            rows.append(jnp.sum(jnp.where(sub == (line & 63), picked, 0.0), axis=0, keepdims=True))
        found.append(jnp.concatenate(rows, axis=0))
    for s in range(4):

        @pl.when(step == s)
        def _():
            values_ref[4 * s : 4 * s + 4, :] = jnp.concatenate(found, axis=1)
            values_ref[16 + 4 * s : 20 + 4 * s, :] = chosen.astype(F32)


def spectra(decayed, right, left, freq, a, b):
    rows = decayed.shape[0]
    full = lambda s: pl.BlockSpec(s, lambda i: (0,) * len(s))
    part = lambda w, j: pl.BlockSpec((256, w), lambda i: (i, j))
    owns = [*a[0], *b[0]]
    flat = [g for done in (a, b) for half in done[1] for g in half]
    return pl.pallas_call(
        spectra_kernel,
        out_shape=[
            jax.ShapeDtypeStruct((rows, 512), F32),
            jax.ShapeDtypeStruct((rows, 512), F32),
            jax.ShapeDtypeStruct((32, 256), F32),
        ],
        grid=(4,),
        in_specs=[part(512, 0), full(right.shape), full(left.shape), pl.BlockSpec((1, 4, 256), lambda i: (i, 0, 0))]
        + [part(128, 3)] * 4
        + [part(128, j) for _, j in flat]
        + [pl.BlockSpec((GROUPS, 128), lambda i, j=j: (rows // GROUPS, j)) for _, j in flat],
        out_specs=[part(512, 0), part(512, 0), full((32, 256))],
        scratch_shapes=[pltpu.VMEM((4, 12, 8, 128), F32)],
        compiler_params=params(20),
        cost_estimate=pl.CostEstimate(flops=10**9, bytes_accessed=16 * 1024 * 1024, transcendentals=0),
    )(decayed, right, left, freq.reshape(4, 4, 256), *owns, *[g for g, _ in flat], *[g for g, _ in flat])


def remove_kernel(moment_ref, spectra_ref, left_ref, right_ref, freq_ref, out_ref):
    sub = lax.broadcasted_iota(jnp.int32, (EDGE, 128), 0)
    for half in range(2):
        cols = slice(half * 256, (half + 1) * 256)
        for block in range(4):
            rows = slice(block * 256, (block + 1) * 256)
            masks = []
            for inner in range(4):
                high, low = pick_rows(freq_ref, block * 4 + inner, half)
                at_low = jnp.where(sub == low, 1.0, 0.0).astype(BF16)
                masks.append(
                    lax.dot_general(
                        at_low, place_matrix(high), (((1,), (1,)), ((), ())), preferred_element_type=F32
                    )
                )
            kept = spectra_ref[rows, cols] * jnp.concatenate(masks, axis=0)
            removed = dot_right(dot_left(left_ref, kept), right_ref)
            out_ref[0, cols, rows] = (moment_ref[rows, cols] - removed).T


def remove(moment, spectrum, left, right, freq):
    rows, cols = moment.shape
    return pl.pallas_call(
        remove_kernel,
        out_shape=jax.ShapeDtypeStruct((1, cols, rows), F32),
        compiler_params=params(24),
        cost_estimate=pl.CostEstimate(flops=10**9, bytes_accessed=6 * 1024 * 1024, transcendentals=0),
    )(moment, spectrum, left, right, freq)


def update_kernel(left_ref, right_ref, *refs):
    lists, (out_ref, values, chosen) = refs[:4], refs[4:]
    step = pl.program_id(0)

    @pl.when(step == 0)
    def _():
        for a in range(8):
            cut = slice(a * PICK, (a + 1) * PICK)
            values[a] = jnp.concatenate([r[o : o + 16, cut] for r in lists for o in (0, 32)], axis=1)
            chosen[a] = jnp.concatenate([r[o : o + 16, cut] for r in lists for o in (16, 48)], axis=1).astype(jnp.int32)

    sub = lax.broadcasted_iota(jnp.int32, (EDGE, 256), 0)
    for group in range(4):
        strips = []
        for inner_a in range(4):
            a = step * 4 + inner_a
            tiles = []
            for inner_b in range(4):
                b = group * 4 + inner_b
                value = values[a, b : b + 1, :]
                where = chosen[a, b : b + 1, :]
                hi, lo = halves(value)
                hit = sub == (where >> 6)
                zero = jnp.zeros((EDGE, 256), F32)
                lhs = jnp.concatenate(
                    [
                        jnp.where(hit, hi.astype(F32), zero).astype(BF16),
                        jnp.where(hit, lo.astype(F32), zero).astype(BF16),
                    ],
                    axis=0,
                )
                rhs = jnp.where(sub == (where & 63), 1.0, 0.0).astype(BF16)
                both = lax.dot_general(lhs, rhs, (((1,), (1,)), ((), ())), preferred_element_type=F32)
                tiles.append(both[:EDGE] + both[EDGE:])
            strips.append(jnp.concatenate(tiles, axis=1))
        spectrum = jnp.concatenate(strips, axis=0)
        out_ref[:, group * 256 : (group + 1) * 256] = dot_right(dot_left(left_ref, spectrum), right_ref) * 0.125


def update_of(lists, left, right):
    full = lambda s: pl.BlockSpec(s, lambda i: (0,) * len(s))
    return pl.pallas_call(
        update_kernel,
        out_shape=jax.ShapeDtypeStruct((512, 1024), F32),
        grid=(2,),
        in_specs=[full(left.shape), full(right.shape)] + [full((64, 256))] * 4,
        out_specs=pl.BlockSpec((256, 1024), lambda i: (i, 0)),
        scratch_shapes=[pltpu.VMEM((8, 16, 256), F32), pltpu.VMEM((8, 16, 256), jnp.int32)],
        compiler_params=params(24),
        cost_estimate=pl.CostEstimate(flops=2 * 10**9, bytes_accessed=3 * 1024 * 1024, transcendentals=0),
    )(left, right, *lists)


def shift(value, axis, by):
    if axis == "x":
        pairs = [(x * 4 + z, (x + by) % 4 * 4 + z) for x in range(4) for z in range(4)]
    else:
        pairs = [(x * 4 + z, x * 4 + (z + by) % 4) for x in range(4) for z in range(4)]
    return lax.ppermute(value, "fsdp", pairs)


def block_table(x, z):
    table = []
    for first, (here, there) in enumerate(((x, z), (z, x))):
        for away in ((2, 2), (3, 1), (1, 3), (0, 0)):
            for spot in range(4):
                for half in range(2):
                    along = (here + away[half]) % RING
                    across = (there + ORDER[half][spot]) % RING
                    dest = 4 * along + across if first == 0 else 4 * across + along
                    table.append(4 * dest + 2 * first + half)
    return jnp.stack(table).astype(jnp.int32)


def both_ways(pair, axis, by):
    return [shift(pair[0], axis, by), shift(pair[1], axis, -by)]


def reduce_half(key, act, table, start, axis):
    other = "z" if axis == "x" else "x"
    run = functools.partial(matmul, key, act, table)
    far = both_ways(run(start, (0, 4)), axis, 1)
    alone = both_ways(run(start + 8, (0, 4)), axis, -1)
    early = both_ways(run(start + 16, (0, 2), far), axis, 1)
    late = both_ways(run(start + 16, (2, 2), far), axis, 1)
    own = run(start + 24, (0, 4), alone, coded=False)
    far = both_ways(fold(own, 0, [[(g, 0)] for g in early]), other, 1)
    last = both_ways(fold(own, 2, [[(g, 0)] for g in late]), other, -1)
    passed = both_ways(fold(own, 1, [[(g, 1), (f, 0)] for g, f in zip(early, far)]), other, 1)
    return own, [[(g, 1), (p, 0), (q, 0)] for g, p, q in zip(late, passed, last)]


def exchange(mine):
    partner = lax.ppermute(mine, "dp", [(i, i ^ 1) for i in range(8)])
    pair = jnp.concatenate([mine, partner], axis=0)
    return [pair] + [
        lax.ppermute(pair, "dp", [(y * 2 + c, (y + by) % 4 * 2 + c) for y in range(4) for c in range(2)])
        for by in (1, 3, 2)
    ]


def per_device(activations, key_cotangent, momentum, frequencies):
    place = lax.axis_index("fsdp")
    x, z = place // RING, place % RING
    cosine = cosine_matrix()
    by_c = jnp.asarray(split_table(np.kron(np.eye(4), cosine)))
    by_ct = jnp.asarray(split_table(np.kron(np.eye(4), cosine.T)))
    decayed = (DECAY * momentum[0]).T
    freq = jnp.transpose(frequencies[0], (1, 0, 2)).reshape(16, 256)
    table = block_table(x, z)
    half_a = reduce_half(key_cotangent, activations, table, 0, "x")
    half_b = reduce_half(key_cotangent, activations, table, 32, "z")
    moment, spectrum, values = spectra(decayed, by_ct, by_c, freq, half_a, half_b)
    lists = exchange(values)
    new_momentum = remove(moment, spectrum, by_ct, by_c, freq)
    update = update_of(lists, by_ct, by_c)
    return update, new_momentum


def solution(mesh):
    in_specs = (
        P(("dp", "fsdp"), None),
        P(("dp", "fsdp"), None),
        P("dp", "fsdp", None),
        P("dp", "fsdp", None, None),
    )
    out_specs = (P("fsdp", None), P("dp", "fsdp", None))
    return jax.shard_map(per_device, mesh=mesh, in_specs=in_specs, out_specs=out_specs, check_vma=False)
```

```python
import functools

import jax
import jax.numpy as jnp
import ml_dtypes
import numpy as np
from jax import lax
from jax.experimental import pallas as pl
from jax.experimental.pallas import tpu as pltpu
from jax.sharding import PartitionSpec as P

EDGE = 64
PICK = 32
DECAY = 0.999
RING = 4
ORDER = ((2, 1, 3, 0), (2, 3, 1, 0))
GROUPS = 16
F32 = jnp.float32
BF16 = jnp.bfloat16


def params(mib):
    return pltpu.CompilerParams(vmem_limit_bytes=mib * 2**20)


def cosine_matrix():
    k = np.arange(EDGE)[:, None]
    n = np.arange(EDGE)[None, :]
    c = np.sqrt(2.0 / EDGE) * np.cos(np.pi * (2 * n + 1) * k / (2 * EDGE))
    c[0] = np.sqrt(1.0 / EDGE)
    return c


def split_table(table, axis):
    hi = table.astype(ml_dtypes.bfloat16)
    lo = (table - hi.astype(np.float64)).astype(ml_dtypes.bfloat16)
    return np.concatenate([hi, hi, lo], axis=axis)


def tables():
    cosine = np.kron(np.eye(4), cosine_matrix())
    return [
        jnp.asarray(split_table(m, axis)) for m, axis in ((cosine, 1), (cosine.T, 0), (cosine.T, 1), (cosine, 0))
    ]


def dot(a, b):
    return jnp.dot(a, b, preferred_element_type=F32)


def halves(a):
    hi = a.astype(BF16)
    return hi, (a - hi.astype(F32)).astype(BF16)


def dot_right(a, table):
    hi, lo = halves(a)
    return dot(jnp.concatenate([hi, lo, hi], axis=1), table[...])


def dot_left(table, a):
    hi, lo = halves(a)
    return dot(table[...], jnp.concatenate([hi, lo, hi], axis=0))


def transform(left, right, blocks):
    done = dot_left(left, jnp.concatenate(blocks, axis=1))
    done = jnp.concatenate([done[:, 256 * n : 256 * (n + 1)] for n in range(len(blocks))], axis=0)
    done = dot_right(done, right)
    return [done[256 * n : 256 * (n + 1)] for n in range(len(blocks))]


def encode(value, out_ref, lanes=slice(None)):
    rows = value.shape[0]
    step = rows // GROUPS
    cube = value.reshape(GROUPS, step, value.shape[1])
    most = jnp.maximum(jnp.max(jnp.abs(cube), axis=1), 1e-30)
    power = jnp.ceil(256.0 * jnp.log2(most) + 0.5)
    inverse = 32767.0 * jnp.exp2(power * (-1.0 / 256.0))
    code = jnp.floor(cube * inverse[:, None, :] + 0.5).astype(jnp.int32).astype(jnp.int16)
    out_ref[:rows, lanes] = code.reshape(rows, value.shape[1])
    out_ref[rows:, lanes] = power.astype(jnp.int32).astype(jnp.int16)


def decode(ref, lanes=slice(None)):
    rows = ref.shape[0] - GROUPS
    step = rows // GROUPS
    scale = jnp.exp2(ref[rows:, lanes].astype(jnp.int32).astype(F32) * (1.0 / 256.0)) * (1.0 / 32767.0)
    code = ref[:rows, lanes].astype(jnp.int32).astype(F32)
    width = code.shape[1]
    return (code.reshape(GROUPS, step, width) * scale[:, None, :]).reshape(rows, width)


SPOTS = 2


def matmul_kernel(coded, extra, table_ref, key_ref, *refs):
    acts, gots, outs = refs[: 2 * SPOTS], refs[2 * SPOTS : 2 * SPOTS + extra], refs[2 * SPOTS + extra :]
    key = key_ref[...]
    for spot in range(SPOTS):
        lanes = slice(spot * 128, (spot + 1) * 128)
        both = jnp.concatenate([r[...] for r in acts[2 * spot : 2 * spot + 2]], axis=1)
        product = lax.dot_general(key, both, (((0,), (0,)), ((), ())), preferred_element_type=F32)
        for half in range(2):
            value = product[:, half * 128 : (half + 1) * 128]
            if extra:
                value = value + decode(gots[half], lanes)
            if coded:
                encode(value, outs[half], lanes)
            else:
                outs[half][:, lanes] = value
                if spot == SPOTS - 1:
                    outs[2 + half][...] = value


def matmul(key, act, table, start, kind, got=(), into=(), grant=48):
    tokens, kv = key.shape
    coded = kind != "own"
    rows = kv + GROUPS if coded else kv
    width = 1024 if kind in ("wide", "last") else 512
    column = lambda n: pl.BlockSpec((tokens, 128), lambda i, t: (0, t[start + 2 * SPOTS * i + n]))
    wide = lambda r, first: pl.BlockSpec((r, SPOTS * 128), lambda i, t: (0, first + i))
    shapes = [jax.ShapeDtypeStruct((rows, width), jnp.int16 if coded else F32)] * 2
    specs = [wide(rows, 2 if kind == "last" else 0)] * 2
    if kind == "own":
        shapes = shapes + [jax.ShapeDtypeStruct((rows, 128), F32)] * 2
        specs = specs + [pl.BlockSpec((rows, 128), lambda i, t: (0, 0))] * 2
    inputs = [key] + [act] * (2 * SPOTS) + list(got)
    body = functools.partial(matmul_kernel, coded, len(got))
    alias = {}
    if into:
        inner, skip = body, 1 + len(inputs)
        body = lambda *refs: inner(*refs[:skip], *refs[skip + 2 :])
        alias = {skip: 0, skip + 1: 1}
    return pl.pallas_call(
        body,
        out_shape=shapes,
        grid_spec=pltpu.PrefetchScalarGridSpec(
            num_scalar_prefetch=1,
            grid=(4 // SPOTS,),
            in_specs=[pl.BlockSpec((tokens, kv), lambda i, t: (0, 0))]
            + [column(n) for n in range(2 * SPOTS)]
            + [wide(kv + GROUPS, 0)] * len(got)
            + [pl.BlockSpec(memory_space=pl.ANY)] * len(into),
            out_specs=specs,
        ),
        input_output_aliases=alias,
        compiler_params=params(grant),
        cost_estimate=pl.CostEstimate(flops=2 * kv * tokens * 1024, bytes_accessed=4 * 2**20, transcendentals=0),
    )(table, *inputs, *into)


def fold_kernel(jobs, counts, *refs):
    refs = list(refs)
    outs = refs[-jobs:]
    for job in range(jobs):
        total = refs.pop(0)[...]
        for _ in range(counts):
            total = total + decode(refs.pop(0))
        encode(total, outs[job])


def fold(jobs, blocks=1, into=None, at=0, width=None, lanes=128):
    rows = jobs[0][0][0].shape[0]
    flat = [entry for job in jobs for entry in job]
    spec = lambda r, j: pl.BlockSpec((r, lanes), lambda i: (0, i + j))
    specs = [spec(a.shape[0], j) for a, j in flat]
    operands = [a for a, _ in flat]
    shape = jax.ShapeDtypeStruct((rows + GROUPS, width or blocks * lanes), jnp.int16)
    alias = {}
    body = functools.partial(fold_kernel, len(jobs), len(jobs[0]) - 1)
    if into is not None:
        shape = jax.ShapeDtypeStruct(into[0].shape, jnp.int16)
        inner, skip = body, len(operands)
        body = lambda *refs: inner(*refs[:skip], *refs[skip + len(into) :])
        alias = {skip + n: n for n in range(len(into))}
        operands = operands + list(into)
        specs = specs + [pl.BlockSpec(memory_space=pl.ANY)] * len(into)
    return pl.pallas_call(
        body,
        out_shape=[shape] * len(jobs),
        grid=(blocks,),
        in_specs=specs,
        out_specs=[spec(rows + GROUPS, at)] * len(jobs),
        input_output_aliases=alias,
        compiler_params=params(10),
        cost_estimate=pl.CostEstimate(flops=rows * 8 * lanes * blocks, bytes_accessed=rows * 8 * lanes * blocks, transcendentals=0),
    )(*operands)


def start_kernel(momentum_ref, *refs):
    owns, out_ref = refs[:4], refs[4]
    for block in range(4):
        lanes = slice(block * 128, (block + 1) * 128)
        out_ref[:, lanes] = (DECAY * momentum_ref[lanes, :]).T + owns[block][...]


def start_of(momentum, owns):
    cols, rows = momentum.shape
    return pl.pallas_call(
        start_kernel,
        out_shape=jax.ShapeDtypeStruct((rows, cols), F32),
        compiler_params=params(12),
        cost_estimate=pl.CostEstimate(flops=10**7, bytes_accessed=6 * 2**20, transcendentals=0),
    )(momentum, *owns)


def base_kernel(start_ref, *refs):
    gots, out_ref = refs[:8], refs[8]
    for block in range(4):
        lanes = slice(block * 128, (block + 1) * 128)
        out_ref[:, lanes] = start_ref[:, lanes] + (decode(gots[2 * block]) + decode(gots[2 * block + 1]))


def base_of(start, lists):
    rows = start.shape[0]
    spec = lambda r, w, j: pl.BlockSpec((r, w), lambda i: (0, j))
    flat = [entry for block in lists for entry in block]
    return pl.pallas_call(
        base_kernel,
        out_shape=jax.ShapeDtypeStruct(start.shape, F32),
        grid=(1,),
        in_specs=[spec(rows, 512, 0)] + [spec(a.shape[0], 128, j) for a, j in flat],
        out_specs=spec(rows, 512, 0),
        compiler_params=params(16),
        cost_estimate=pl.CostEstimate(flops=10**7, bytes_accessed=6 * 2**20, transcendentals=0),
    )(start, *[a for a, _ in flat])


def pick_rows(freq_ref, b, half):
    chosen = freq_ref[b : b + 1, half * 128 : (half + 1) * 128]
    return chosen >> 6, chosen & 63


def place_matrix(high):
    tile = lax.broadcasted_iota(jnp.int32, (1, 128), 1) // PICK
    rows = lax.broadcasted_iota(jnp.int32, (256, 128), 0)
    return jnp.where(rows == high + tile * EDGE, 1.0, 0.0).astype(BF16)


def spectra_kernel(base_ref, right_ref, left_ref, freq_ref, *refs):
    gots, scales = refs[:8], refs[8:16]
    moment_ref, spectra_ref, values_ref, scale = refs[16:]
    step = pl.program_id(0)
    tiles = base_ref.shape[0] // EDGE

    @pl.when(step == 0)
    def _():
        for j, s in enumerate(scales):
            unit = jnp.exp2(s[...].astype(jnp.int32).astype(F32) * (1.0 / 256.0)) * (1.0 / 32767.0)
            for c in range(GROUPS // tiles):
                scale[c, j] = unit[tiles * c : tiles * (c + 1)]

    sub = lax.broadcasted_iota(jnp.int32, (EDGE, 128), 0)
    chosen = freq_ref[0]
    moments = {}
    for half in range(2):
        parts = []
        for block in (2 * half, 2 * half + 1):
            total = base_ref[:, block * 128 : (block + 1) * 128]
            for j in range(2 * block, 2 * block + 2):
                code = gots[j][...].astype(jnp.int32).astype(F32).reshape(tiles, EDGE, 128)
                total = total + (code * scale[step, j][:, None, :]).reshape(tiles * EDGE, 128)
            parts.append(total)
        moment = jnp.concatenate(parts, axis=1)
        moment_ref[:, half * 256 : (half + 1) * 256] = moment
        for block in range(tiles // 4):
            moments[block, half] = moment[block * 256 : (block + 1) * 256]
    spectrums = dict(zip(moments, transform(left_ref, right_ref, list(moments.values()))))
    found = []
    for half in range(2):
        rows = []
        for tile in range(tiles):
            block, inner = tile // 4, tile % 4
            spectrum = spectrums[block, half][inner * EDGE : (inner + 1) * EDGE]
            spectra_ref[tile * EDGE : (tile + 1) * EDGE, half * 256 : (half + 1) * 256] = spectrum
            hi, lo = halves(spectrum)
            line = chosen[tile : tile + 1, half * 128 : (half + 1) * 128]
            place = place_matrix(line >> 6)
            picked = dot(jnp.concatenate([hi, lo], axis=0), place)
            picked = picked[:EDGE] + picked[EDGE:]
            rows.append(jnp.sum(jnp.where(sub == (line & 63), picked, 0.0), axis=0, keepdims=True))
        found.append(jnp.concatenate(rows, axis=0))
    for s in range(GROUPS // tiles):

        @pl.when(step == s)
        def _():
            values_ref[tiles * s : tiles * (s + 1), :] = jnp.concatenate(found, axis=1)
            values_ref[16 + tiles * s : 16 + tiles * (s + 1), :] = chosen.astype(F32)


def spectra(base, right, left, freq, lists):
    rows = base.shape[0]
    part_rows = 512
    steps = rows // part_rows
    full = lambda s: pl.BlockSpec(s, lambda i: (0,) * len(s))
    part = lambda w, j: pl.BlockSpec((part_rows, w), lambda i: (i, j))
    flat = [entry for block in lists for entry in block]
    return pl.pallas_call(
        spectra_kernel,
        out_shape=[
            jax.ShapeDtypeStruct((rows, 512), F32),
            jax.ShapeDtypeStruct((rows, 512), F32),
            jax.ShapeDtypeStruct((32, 256), F32),
        ],
        grid=(steps,),
        in_specs=[part(512, 0), full(right.shape), full(left.shape), pl.BlockSpec((1, GROUPS // steps, 256), lambda i: (i, 0, 0))]
        + [part(128, j) for _, j in flat]
        + [pl.BlockSpec((GROUPS, 128), lambda i, j=j: (rows // GROUPS, j)) for _, j in flat],
        out_specs=[part(512, 0), part(512, 0), full((32, 256))],
        scratch_shapes=[pltpu.VMEM((steps, 8, GROUPS // steps, 128), F32)],
        compiler_params=params(24),
        cost_estimate=pl.CostEstimate(flops=10**9, bytes_accessed=8 * 2**20, transcendentals=0),
    )(base, right, left, freq.reshape(steps, GROUPS // steps, 256), *[g for g, _ in flat], *[g for g, _ in flat])


def remove_kernel(moment_ref, spectra_ref, left_ref, right_ref, freq_ref, out_ref):
    sub = lax.broadcasted_iota(jnp.int32, (EDGE, 128), 0)
    places = [
        (slice(block * 256, (block + 1) * 256), slice(half * 256, (half + 1) * 256))
        for half in range(2)
        for block in range(4)
    ]
    for some in (places[:4], places[4:]):
        kept = []
        for rows, cols in some:
            masks = []
            for inner in range(4):
                high, low = pick_rows(freq_ref, rows.start // EDGE + inner, cols.start // 256)
                at_low = jnp.where(sub == low, 1.0, 0.0).astype(BF16)
                masks.append(
                    lax.dot_general(
                        at_low, place_matrix(high), (((1,), (1,)), ((), ())), preferred_element_type=F32
                    )
                )
            kept.append(spectra_ref[rows, cols] * jnp.concatenate(masks, axis=0))
        for (rows, cols), removed in zip(some, transform(left_ref, right_ref, kept)):
            out_ref[0, cols, rows] = (moment_ref[rows, cols] - removed).T


def remove(moment, spectrum, left, right, freq):
    rows, cols = moment.shape
    return pl.pallas_call(
        remove_kernel,
        out_shape=jax.ShapeDtypeStruct((1, cols, rows), F32),
        compiler_params=params(24),
        cost_estimate=pl.CostEstimate(flops=10**9, bytes_accessed=6 * 1024 * 1024, transcendentals=0),
    )(moment, spectrum, left, right, freq)


def update_kernel(left_ref, right_ref, *refs):
    lists, (out_ref, values, chosen) = refs[:4], refs[4:]
    step = pl.program_id(0)

    @pl.when(step == 0)
    def _():
        for a in range(8):
            cut = slice(a * PICK, (a + 1) * PICK)
            values[a] = jnp.concatenate([r[o : o + 16, cut] for r in lists for o in (0, 32)], axis=1)
            chosen[a] = jnp.concatenate([r[o : o + 16, cut] for r in lists for o in (16, 48)], axis=1).astype(jnp.int32)

    sub = lax.broadcasted_iota(jnp.int32, (EDGE, 256), 0)
    spectrums = []
    for group in range(4):
        strips = []
        for inner_a in range(4):
            a = step * 4 + inner_a
            tiles = []
            for inner_b in range(4):
                b = group * 4 + inner_b
                value = values[a, b : b + 1, :]
                where = chosen[a, b : b + 1, :]
                hi, lo = halves(value)
                hit = sub == (where >> 6)
                zero = jnp.zeros((EDGE, 256), F32)
                lhs = jnp.concatenate(
                    [
                        jnp.where(hit, hi.astype(F32), zero).astype(BF16),
                        jnp.where(hit, lo.astype(F32), zero).astype(BF16),
                    ],
                    axis=0,
                )
                rhs = jnp.where(sub == (where & 63), 1.0, 0.0).astype(BF16)
                both = lax.dot_general(lhs, rhs, (((1,), (1,)), ((), ())), preferred_element_type=F32)
                tiles.append(both[:EDGE] + both[EDGE:])
            strips.append(jnp.concatenate(tiles, axis=1))
        spectrums.append(jnp.concatenate(strips, axis=0))
    for group, done in enumerate(transform(left_ref, right_ref, spectrums)):
        out_ref[:, group * 256 : (group + 1) * 256] = done * 0.125


def update_of(lists, left, right):
    full = lambda s: pl.BlockSpec(s, lambda i: (0,) * len(s))
    return pl.pallas_call(
        update_kernel,
        out_shape=jax.ShapeDtypeStruct((512, 1024), F32),
        grid=(2,),
        in_specs=[full(left.shape), full(right.shape)] + [full((64, 256))] * 4,
        out_specs=pl.BlockSpec((256, 1024), lambda i: (i, 0)),
        scratch_shapes=[pltpu.VMEM((8, 16, 256), F32), pltpu.VMEM((8, 16, 256), jnp.int32)],
        compiler_params=params(24),
        cost_estimate=pl.CostEstimate(flops=2 * 10**9, bytes_accessed=3 * 1024 * 1024, transcendentals=0),
    )(left, right, *lists)


def shift(value, axis, by):
    if axis == "x":
        pairs = [(x * 4 + z, (x + by) % 4 * 4 + z) for x in range(4) for z in range(4)]
    else:
        pairs = [(x * 4 + z, x * 4 + (z + by) % 4) for x in range(4) for z in range(4)]
    return lax.ppermute(value, "fsdp", pairs)


def block_table(x, z):
    table = []
    for first, (here, there) in enumerate(((x, z), (z, x))):
        for away in ((2, 2), (3, 1), (1, 3), (0, 0)):
            for spot in range(4):
                for half in range(2):
                    along = (here + away[half]) % RING
                    across = (there + ORDER[half][spot]) % RING
                    dest = 4 * along + across if first == 0 else 4 * across + along
                    table.append(4 * dest + 2 * first + half)
    return jnp.stack(table).astype(jnp.int32)


def both_ways(pair, axis, by):
    return [shift(pair[0], axis, by), shift(pair[1], axis, -by)]


def stage_one(key, act, table):
    run = functools.partial(matmul, key, act)
    far_a = both_ways(run(table, 0, "coded", grant=48), "x", 1)
    far_b = both_ways(run(table, 32, "coded"), "z", 1)
    alone_a = run(table, 8, "wide")
    alone_b = run(table, 40, "wide")
    far_a, alone_b = lax.optimization_barrier((far_a, alone_b))
    out_a = run(table, 16, "last", far_a, alone_a[::-1])
    out_a, table = lax.optimization_barrier((out_a, table))
    got_a = both_ways(out_a, "x", 1)
    out_b = run(table, 48, "last", far_b, alone_b[::-1])
    out_b, table = lax.optimization_barrier((out_b, table))
    got_b = both_ways(out_b, "z", 1)
    return got_a, got_b, run(table, 24, "own"), run(table, 56, "own")


def stage_two(own, up, down, axis):
    def heard(spot):
        return [(up, 4 + spot), (down, spot)], [(down, 4 + spot), (up, spot)]

    def sums(spot):
        return [[(own[half], spot)] + heard(spot)[half] for half in range(2)]

    far = both_ways(fold(sums(0)), axis, 1)
    alone = fold(sums(2), width=256)
    middle = sums(1)
    sent = fold([middle[n] + [(far[n], 0)] for n in range(2)], 1, alone[::-1], 1)
    return list(heard(3)), sent


def sum_of(got):
    up, down = got
    return [[(up, 1), (down, 0)], [(down, 1), (up, 0)]]


def exchange(mine):
    partner = lax.ppermute(mine, "dp", [(i, i ^ 1) for i in range(8)])
    pair = jnp.concatenate([mine, partner], axis=0)
    return [pair] + [
        lax.ppermute(pair, "dp", [(y * 2 + c, (y + by) % 4 * 2 + c) for y in range(4) for c in range(2)])
        for by in (1, 3, 2)
    ]


def per_device(activations, key_cotangent, momentum, frequencies):
    place = lax.axis_index("fsdp")
    x, z = place // RING, place % RING
    there_left, there_right, back_left, back_right = tables()
    freq = jnp.transpose(frequencies[0], (1, 0, 2)).reshape(16, 256)
    table = block_table(x, z)
    one_a, one_b, own_a, own_b = stage_one(key_cotangent, activations, table)
    start = start_of(momentum[0], own_a[2:] + own_b[2:])
    own_a, own_b, start, freq = lax.optimization_barrier((own_a, own_b, start, freq))
    half_a, sent_a = stage_two(own_a, *one_a, "z")
    one_b, sent_a = lax.optimization_barrier((one_b, sent_a))
    half_a = (half_a, sum_of(both_ways(sent_a, "z", 1)))
    half_b, sent_b = stage_two(own_b, *one_b, "x")
    half_b = (half_b, sum_of(both_ways(sent_b, "x", 1)))
    base = base_of(start, half_a[0] + half_b[0])
    moment, spectrum, values = spectra(base, there_right, there_left, freq, half_a[1] + half_b[1])
    lists = exchange(values)
    new_momentum = remove(moment, spectrum, back_left, back_right, freq)
    update = update_of(lists, back_left, back_right)
    return update, new_momentum


def solution(mesh):
    in_specs = (
        P(("dp", "fsdp"), None),
        P(("dp", "fsdp"), None),
        P("dp", "fsdp", None),
        P("dp", "fsdp", None, None),
    )
    out_specs = (P("fsdp", None), P("dp", "fsdp", None))
    return jax.shard_map(per_device, mesh=mesh, in_specs=in_specs, out_specs=out_specs, check_vma=False)
```

```python
import functools

import jax
import jax.numpy as jnp
import ml_dtypes
import numpy as np
from jax import lax
from jax.experimental import pallas as pl
from jax.experimental.pallas import tpu as pltpu
from jax.sharding import PartitionSpec as P

EDGE = 64
PICK = 32
DECAY = 0.999
RING = 4
ORDER = ((2, 1, 3, 0), (2, 3, 1, 0))
PART = 1024
GROUPS = 16
F32 = jnp.float32
BF16 = jnp.bfloat16


def params(mib):
    return pltpu.CompilerParams(vmem_limit_bytes=mib * 2**20)


def cosine_matrix():
    k = np.arange(EDGE)[:, None]
    n = np.arange(EDGE)[None, :]
    c = np.sqrt(2.0 / EDGE) * np.cos(np.pi * (2 * n + 1) * k / (2 * EDGE))
    c[0] = np.sqrt(1.0 / EDGE)
    return c


def split_table(table, axis):
    hi = table.astype(ml_dtypes.bfloat16)
    lo = (table - hi.astype(np.float64)).astype(ml_dtypes.bfloat16)
    return np.concatenate([hi, hi, lo], axis=axis)


def tables():
    cosine = np.kron(np.eye(4), cosine_matrix())
    return [
        jnp.asarray(split_table(m, axis)) for m, axis in ((cosine, 1), (cosine.T, 0), (cosine.T, 1), (cosine, 0))
    ]


def dot(a, b):
    return jnp.dot(a, b, preferred_element_type=F32)


def halves(a):
    hi = a.astype(BF16)
    return hi, (a - hi.astype(F32)).astype(BF16)


def dot_right(a, table):
    hi, lo = halves(a)
    return dot(jnp.concatenate([hi, lo, hi], axis=1), table[...])


def dot_left(table, a):
    hi, lo = halves(a)
    return dot(table[...], jnp.concatenate([hi, lo, hi], axis=0))


def transform(left, right, blocks):
    done = dot_left(left, jnp.concatenate(blocks, axis=1))
    done = jnp.concatenate([done[:, 256 * n : 256 * (n + 1)] for n in range(len(blocks))], axis=0)
    done = dot_right(done, right)
    return [done[256 * n : 256 * (n + 1)] for n in range(len(blocks))]


def encode(value, out_ref, lanes=slice(None)):
    rows = value.shape[0]
    step = rows // GROUPS
    cube = value.reshape(GROUPS, step, value.shape[1])
    most = jnp.maximum(jnp.max(jnp.abs(cube), axis=1), 1e-30)
    power = jnp.ceil(256.0 * jnp.log2(most) + 0.5)
    inverse = 32767.0 * jnp.exp2(power * (-1.0 / 256.0))
    code = jnp.floor(cube * inverse[:, None, :] + 0.5).astype(jnp.int32).astype(jnp.int16)
    out_ref[:rows, lanes] = code.reshape(rows, value.shape[1])
    out_ref[rows:, lanes] = power.astype(jnp.int32).astype(jnp.int16)


def decode(ref, lanes=slice(None)):
    rows = ref.shape[0] - GROUPS
    step = rows // GROUPS
    scale = jnp.exp2(ref[rows:, lanes].astype(jnp.int32).astype(F32) * (1.0 / 256.0)) * (1.0 / 32767.0)
    code = ref[:rows, lanes].astype(jnp.int32).astype(F32)
    width = code.shape[1]
    return (code.reshape(GROUPS, step, width) * scale[:, None, :]).reshape(rows, width)


SPOTS = 2


def matmul_kernel(coded, extra, table_ref, key_ref, *refs):
    acts, gots, outs = refs[: 2 * SPOTS], refs[2 * SPOTS : 2 * SPOTS + extra], refs[2 * SPOTS + extra :]
    key = key_ref[...]
    for spot in range(SPOTS):
        lanes = slice(spot * 128, (spot + 1) * 128)
        both = jnp.concatenate([r[...] for r in acts[2 * spot : 2 * spot + 2]], axis=1)
        product = lax.dot_general(key, both, (((0,), (0,)), ((), ())), preferred_element_type=F32)
        for half in range(2):
            value = product[:, half * 128 : (half + 1) * 128]
            if extra:
                value = value + decode(gots[half], lanes)
            if coded:
                encode(value, outs[half], lanes)
            else:
                outs[half][:, lanes] = value
                if spot == SPOTS - 1:
                    outs[2 + half][...] = value


def matmul(key, act, table, start, kind, got=(), into=(), grant=48):
    tokens, kv = key.shape
    coded = kind != "own"
    rows = kv + GROUPS if coded else kv
    width = 1024 if kind in ("wide", "last") else 512
    column = lambda n: pl.BlockSpec((tokens, 128), lambda i, t: (0, t[start + 2 * SPOTS * i + n]))
    wide = lambda r, first: pl.BlockSpec((r, SPOTS * 128), lambda i, t: (0, first + i))
    shapes = [jax.ShapeDtypeStruct((rows, width), jnp.int16 if coded else F32)] * 2
    specs = [wide(rows, 2 if kind == "last" else 0)] * 2
    if kind == "own":
        shapes = shapes + [jax.ShapeDtypeStruct((rows, 128), F32)] * 2
        specs = specs + [pl.BlockSpec((rows, 128), lambda i, t: (0, 0))] * 2
    inputs = [key] + [act] * (2 * SPOTS) + list(got)
    body = functools.partial(matmul_kernel, coded, len(got))
    alias = {}
    if into:
        inner, skip = body, 1 + len(inputs)
        body = lambda *refs: inner(*refs[:skip], *refs[skip + 2 :])
        alias = {skip: 0, skip + 1: 1}
    return pl.pallas_call(
        body,
        out_shape=shapes,
        grid_spec=pltpu.PrefetchScalarGridSpec(
            num_scalar_prefetch=1,
            grid=(4 // SPOTS,),
            in_specs=[pl.BlockSpec((tokens, kv), lambda i, t: (0, 0))]
            + [column(n) for n in range(2 * SPOTS)]
            + [wide(kv + GROUPS, 0)] * len(got)
            + [pl.BlockSpec(memory_space=pl.ANY)] * len(into),
            out_specs=specs,
        ),
        input_output_aliases=alias,
        compiler_params=params(grant),
        cost_estimate=pl.CostEstimate(flops=2 * kv * tokens * 1024, bytes_accessed=4 * 2**20, transcendentals=0),
    )(table, *inputs, *into)


def fold_kernel(jobs, counts, *refs):
    refs = list(refs)
    outs = refs[-jobs:]
    for job in range(jobs):
        total = refs.pop(0)[...]
        for _ in range(counts):
            total = total + decode(refs.pop(0))
        encode(total, outs[job])


def fold(jobs, blocks=1, into=None, at=0, width=None, lanes=128):
    rows = jobs[0][0][0].shape[0]
    flat = [entry for job in jobs for entry in job]
    spec = lambda r, j: pl.BlockSpec((r, lanes), lambda i: (0, i + j))
    specs = [spec(a.shape[0], j) for a, j in flat]
    operands = [a for a, _ in flat]
    shape = jax.ShapeDtypeStruct((rows + GROUPS, width or blocks * lanes), jnp.int16)
    alias = {}
    body = functools.partial(fold_kernel, len(jobs), len(jobs[0]) - 1)
    if into is not None:
        shape = jax.ShapeDtypeStruct(into[0].shape, jnp.int16)
        inner, skip = body, len(operands)
        body = lambda *refs: inner(*refs[:skip], *refs[skip + len(into) :])
        alias = {skip + n: n for n in range(len(into))}
        operands = operands + list(into)
        specs = specs + [pl.BlockSpec(memory_space=pl.ANY)] * len(into)
    return pl.pallas_call(
        body,
        out_shape=[shape] * len(jobs),
        grid=(blocks,),
        in_specs=specs,
        out_specs=[spec(rows + GROUPS, at)] * len(jobs),
        input_output_aliases=alias,
        compiler_params=params(10),
        cost_estimate=pl.CostEstimate(flops=rows * 8 * lanes * blocks, bytes_accessed=rows * 8 * lanes * blocks, transcendentals=0),
    )(*operands)


def start_kernel(momentum_ref, *refs):
    owns, out_ref = refs[:4], refs[4]
    for block in range(4):
        lanes = slice(block * 128, (block + 1) * 128)
        out_ref[:, lanes] = (DECAY * momentum_ref[lanes, :]).T + owns[block][...]


def start_of(momentum, owns):
    cols, rows = momentum.shape
    return pl.pallas_call(
        start_kernel,
        out_shape=jax.ShapeDtypeStruct((rows, cols), F32),
        compiler_params=params(12),
        cost_estimate=pl.CostEstimate(flops=10**7, bytes_accessed=6 * 2**20, transcendentals=0),
    )(momentum, *owns)


def base_kernel(start_ref, *refs):
    gots, out_ref = refs[:8], refs[8]
    for block in range(4):
        lanes = slice(block * 128, (block + 1) * 128)
        out_ref[:, lanes] = start_ref[:, lanes] + (decode(gots[2 * block]) + decode(gots[2 * block + 1]))


def base_of(start, lists):
    rows = start.shape[0]
    spec = lambda r, w, j: pl.BlockSpec((r, w), lambda i: (0, j))
    flat = [entry for block in lists for entry in block]
    return pl.pallas_call(
        base_kernel,
        out_shape=jax.ShapeDtypeStruct(start.shape, F32),
        grid=(1,),
        in_specs=[spec(rows, 512, 0)] + [spec(a.shape[0], 128, j) for a, j in flat],
        out_specs=spec(rows, 512, 0),
        compiler_params=params(16),
        cost_estimate=pl.CostEstimate(flops=10**7, bytes_accessed=6 * 2**20, transcendentals=0),
    )(start, *[a for a, _ in flat])


def pick_rows(freq_ref, b, half):
    chosen = freq_ref[b : b + 1, half * 128 : (half + 1) * 128]
    return chosen >> 6, chosen & 63


def place_matrix(high):
    tile = lax.broadcasted_iota(jnp.int32, (1, 128), 1) // PICK
    rows = lax.broadcasted_iota(jnp.int32, (256, 128), 0)
    return jnp.where(rows == high + tile * EDGE, 1.0, 0.0).astype(BF16)


def spectra_kernel(final, base_ref, right_ref, left_ref, freq_ref, *refs):
    gots, scales, refs = refs[:4], refs[4:8], refs[8:]
    if final:
        whole_ref, before_ref, refs = refs[0], refs[1], refs[2:]
    moment_ref, spectra_ref, list_ref, scale = refs
    step = pl.program_id(0)
    tiles = base_ref.shape[0] // EDGE

    @pl.when(step == 0)
    def _():
        for j, s in enumerate(scales):
            unit = jnp.exp2(s[...].astype(jnp.int32).astype(F32) * (1.0 / 256.0)) * (1.0 / 32767.0)
            for c in range(GROUPS // tiles):
                scale[c, j] = unit[tiles * c : tiles * (c + 1)]
        if final:
            list_ref[:16, :128] = before_ref[...]
            list_ref[16:, :] = whole_ref[...].astype(F32)

    sub = lax.broadcasted_iota(jnp.int32, (EDGE, 128), 0)
    chosen = freq_ref[0]
    parts = []
    for block in range(2):
        total = base_ref[:, block * 128 : (block + 1) * 128]
        for j in range(2 * block, 2 * block + 2):
            code = gots[j][...].astype(jnp.int32).astype(F32).reshape(tiles, EDGE, 128)
            total = total + (code * scale[step, j][:, None, :]).reshape(tiles * EDGE, 128)
        parts.append(total)
    moment = jnp.concatenate(parts, axis=1)
    moment_ref[...] = moment
    spectrums = transform(left_ref, right_ref, [moment[n : n + 256] for n in range(0, tiles * EDGE, 256)])
    rows = []
    for tile in range(tiles):
        spectrum = spectrums[tile // 4][tile % 4 * EDGE : (tile % 4 + 1) * EDGE]
        spectra_ref[tile * EDGE : (tile + 1) * EDGE, :] = spectrum
        hi, lo = halves(spectrum)
        line = chosen[tile : tile + 1, :]
        picked = dot(jnp.concatenate([hi, lo], axis=0), place_matrix(line >> 6))
        picked = picked[:EDGE] + picked[EDGE:]
        rows.append(jnp.sum(jnp.where(sub == (line & 63), picked, 0.0), axis=0, keepdims=True))
    found = jnp.concatenate(rows, axis=0)
    for s in range(GROUPS // tiles):

        @pl.when(step == s)
        def _():
            if final:
                list_ref[tiles * s : tiles * (s + 1), 128:] = found
            else:
                list_ref[tiles * s : tiles * (s + 1), :] = found


def spectra(base, right, left, freq, lists, half, before=None):
    rows = base.shape[0]
    part_rows = PART
    steps = rows // part_rows
    tiles = GROUPS // steps
    full = lambda s: pl.BlockSpec(s, lambda i: (0,) * len(s))
    part = lambda w, j: pl.BlockSpec((part_rows, w), lambda i: (i, j))
    flat = [entry for block in lists for entry in block]
    final = before is not None
    shape = (32, 256) if final else (16, 128)
    return pl.pallas_call(
        functools.partial(spectra_kernel, final),
        out_shape=[
            jax.ShapeDtypeStruct((rows, 256), F32),
            jax.ShapeDtypeStruct((rows, 256), F32),
            jax.ShapeDtypeStruct(shape, F32),
        ],
        grid=(steps,),
        in_specs=[part(256, half), full(right.shape), full(left.shape), pl.BlockSpec((1, tiles, 128), lambda i: (i, 0, half))]
        + [part(128, j) for _, j in flat]
        + [pl.BlockSpec((GROUPS, 128), lambda i, j=j: (rows // GROUPS, j)) for _, j in flat]
        + ([full((16, 256)), full((16, 128))] if final else []),
        out_specs=[part(256, 0), part(256, 0), full(shape)],
        scratch_shapes=[pltpu.VMEM((steps, 4, tiles, 128), F32)],
        compiler_params=params(20),
        cost_estimate=pl.CostEstimate(flops=10**9, bytes_accessed=4 * 2**20, transcendentals=0),
    )(
        *[base, right, left, freq.reshape(steps, tiles, 256)],
        *[g for g, _ in flat] * 2,
        *([freq, before] if final else []),
    )


def remove_kernel(half, moment_ref, spectra_ref, left_ref, right_ref, freq_ref, *refs):
    out_ref = refs[-1]
    sub = lax.broadcasted_iota(jnp.int32, (EDGE, 128), 0)
    kept = []
    for block in range(4):
        masks = []
        for inner in range(4):
            high, low = pick_rows(freq_ref, block * 4 + inner, half)
            at_low = jnp.where(sub == low, 1.0, 0.0).astype(BF16)
            masks.append(
                lax.dot_general(at_low, place_matrix(high), (((1,), (1,)), ((), ())), preferred_element_type=F32)
            )
        kept.append(spectra_ref[block * 256 : (block + 1) * 256] * jnp.concatenate(masks, axis=0))
    for block, removed in enumerate(transform(left_ref, right_ref, kept)):
        rows = slice(block * 256, (block + 1) * 256)
        out_ref[0, :, rows] = (moment_ref[rows] - removed).T


def remove(moment, spectrum, left, right, freq, half, into=None):
    rows = moment.shape[0]
    full = lambda s: pl.BlockSpec(s, lambda i: (0,) * len(s))
    operands = [moment, spectrum, left, right, freq]
    specs = [full(a.shape) for a in operands]
    if into is not None:
        operands.append(into)
        specs.append(pl.BlockSpec(memory_space=pl.ANY))
    return pl.pallas_call(
        functools.partial(remove_kernel, half),
        out_shape=jax.ShapeDtypeStruct((1, 512, rows), F32),
        grid=(1,),
        in_specs=specs,
        out_specs=pl.BlockSpec((1, 256, rows), lambda i: (0, half, 0)),
        input_output_aliases={} if into is None else {5: 0},
        compiler_params=params(20),
        cost_estimate=pl.CostEstimate(flops=10**9, bytes_accessed=4 * 2**20, transcendentals=0),
    )(*operands)


def update_kernel(left_ref, right_ref, *refs):
    lists, (out_ref,) = refs[:4], refs[4:]
    values, chosen = [], []
    for a in range(8):
        cut = slice(a * PICK, (a + 1) * PICK)
        values.append(jnp.concatenate([r[o : o + 16, cut] for r in lists for o in (0, 32)], axis=1))
        chosen.append(jnp.concatenate([r[o : o + 16, cut] for r in lists for o in (16, 48)], axis=1).astype(jnp.int32))

    sub = lax.broadcasted_iota(jnp.int32, (EDGE, 256), 0)
    zero = jnp.zeros((EDGE, 256), F32)

    def tile(a, b):
        hi, lo = halves(values[a][b : b + 1, :])
        where = chosen[a][b : b + 1, :]
        hit = sub == (where >> 6)
        parts = [jnp.where(hit, part.astype(F32), zero).astype(BF16) for part in (hi, lo)]
        rhs = jnp.where(sub == (where & 63), 1.0, 0.0).astype(BF16)
        both = lax.dot_general(
            jnp.concatenate(parts, axis=0), rhs, (((1,), (1,)), ((), ())), preferred_element_type=F32
        )
        return both[:EDGE] + both[EDGE:]

    for some in range(2):
        spectrums = []
        for group in range(4):
            strips = [
                jnp.concatenate([tile(some * 4 + a, group * 4 + b) for b in range(4)], axis=1) for a in range(4)
            ]
            spectrums.append(jnp.concatenate(strips, axis=0))
        for group, done in enumerate(transform(left_ref, right_ref, spectrums)):
            out_ref[some * 256 : (some + 1) * 256, group * 256 : (group + 1) * 256] = done * 0.125


def update_of(lists, left, right):
    full = lambda s: pl.BlockSpec(s, lambda i: (0,) * len(s))
    return pl.pallas_call(
        update_kernel,
        out_shape=jax.ShapeDtypeStruct((512, 1024), F32),
        grid=(1,),
        in_specs=[full(left.shape), full(right.shape)] + [full((64, 256))] * 4,
        out_specs=full((512, 1024)),
        compiler_params=params(24),
        cost_estimate=pl.CostEstimate(flops=2 * 10**9, bytes_accessed=3 * 1024 * 1024, transcendentals=0),
    )(left, right, *lists)


def shift(value, axis, by):
    if axis == "x":
        pairs = [(x * 4 + z, (x + by) % 4 * 4 + z) for x in range(4) for z in range(4)]
    else:
        pairs = [(x * 4 + z, x * 4 + (z + by) % 4) for x in range(4) for z in range(4)]
    return lax.ppermute(value, "fsdp", pairs)


def block_table(x, z):
    table = []
    for first, (here, there) in enumerate(((x, z), (z, x))):
        for away in ((2, 2), (3, 1), (1, 3), (0, 0)):
            for spot in range(4):
                for half in range(2):
                    along = (here + away[half]) % RING
                    across = (there + ORDER[half][spot]) % RING
                    dest = 4 * along + across if first == 0 else 4 * across + along
                    table.append(4 * dest + 2 * first + half)
    return jnp.stack(table).astype(jnp.int32)


def both_ways(pair, axis, by):
    return [shift(pair[0], axis, by), shift(pair[1], axis, -by)]


def stage_one(key, act, table):
    run = functools.partial(matmul, key, act)
    far_a = both_ways(run(table, 0, "coded", grant=48), "x", 1)
    far_b = both_ways(run(table, 32, "coded"), "z", 1)
    alone_a = run(table, 8, "wide")
    alone_b = run(table, 40, "wide")
    far_a, alone_b = lax.optimization_barrier((far_a, alone_b))
    out_a = run(table, 16, "last", far_a, alone_a[::-1])
    out_a, table = lax.optimization_barrier((out_a, table))
    got_a = both_ways(out_a, "x", 1)
    out_b = run(table, 48, "last", far_b, alone_b[::-1])
    out_b, table = lax.optimization_barrier((out_b, table))
    got_b = both_ways(out_b, "z", 1)
    return got_a, got_b, run(table, 24, "own"), run(table, 56, "own")


def stage_two(own, up, down, axis):
    def heard(spot):
        return [(up, 4 + spot), (down, spot)], [(down, 4 + spot), (up, spot)]

    def sums(spot):
        return [[(own[half], spot)] + heard(spot)[half] for half in range(2)]

    far = both_ways(fold(sums(0)), axis, 1)
    alone = fold(sums(2), width=256)
    middle = sums(1)
    sent = fold([middle[n] + [(far[n], 0)] for n in range(2)], 1, alone[::-1], 1)
    return list(heard(3)), sent


def sum_of(got):
    up, down = got
    return [[(up, 1), (down, 0)], [(down, 1), (up, 0)]]


def exchange(mine):
    partner = lax.ppermute(mine, "dp", [(i, i ^ 1) for i in range(8)])
    pair = jnp.concatenate([mine, partner], axis=0)
    return [pair] + [
        lax.ppermute(pair, "dp", [(y * 2 + c, (y + by) % 4 * 2 + c) for y in range(4) for c in range(2)])
        for by in (1, 3, 2)
    ]


def per_device(activations, key_cotangent, momentum, frequencies):
    place = lax.axis_index("fsdp")
    x, z = place // RING, place % RING
    there_left, there_right, back_left, back_right = tables()
    freq = jnp.transpose(frequencies[0], (1, 0, 2)).reshape(16, 256)
    table = block_table(x, z)
    one_a, one_b, own_a, own_b = stage_one(key_cotangent, activations, table)
    start = start_of(momentum[0], own_a[2:] + own_b[2:])
    own_a, own_b, start, freq = lax.optimization_barrier((own_a, own_b, start, freq))
    half_a, sent_a = stage_two(own_a, *one_a, "z")
    one_b, sent_a = lax.optimization_barrier((one_b, sent_a))
    last_a = both_ways(sent_a, "z", 1)
    half_b, sent_b = stage_two(own_b, *one_b, "x")
    last_b = both_ways(sent_b, "x", 1)
    base = base_of(start, half_a + half_b)
    moment, spectrum, values = spectra(base, there_right, there_left, freq, sum_of(last_a), 0)
    new_momentum = remove(moment, spectrum, back_left, back_right, freq, 0)
    last_b, values, new_momentum = lax.optimization_barrier((last_b, values, new_momentum))
    moment, spectrum, mine = spectra(base, there_right, there_left, freq, sum_of(last_b), 1, values)
    lists = exchange(mine)
    new_momentum = remove(moment, spectrum, back_left, back_right, freq, 1, new_momentum)
    update = update_of(lists, back_left, back_right)
    return update, new_momentum


def solution(mesh):
    in_specs = (
        P(("dp", "fsdp"), None),
        P(("dp", "fsdp"), None),
        P("dp", "fsdp", None),
        P("dp", "fsdp", None, None),
    )
    out_specs = (P("fsdp", None), P("dp", "fsdp", None))
    return jax.shard_map(per_device, mesh=mesh, in_specs=in_specs, out_specs=out_specs, check_vma=False)
```
